256 devices in a mesh: rep: 4 (over x_hi, core), shard: 64 (over z, x_lo, y).
Axes of the slice: x: 4 (x_hi: 2, x_lo: 2; x = x_hi * 2 + x_lo), y: 4, z: 8, core: 2. Of those that a mesh axis runs over, the one named last changes fastest.
Arguments:
- activations: bfloat16 [2, 65536, 4096], P(None, ('rep', 'shard')), may hold values from -6 to 6
- output_grad: bfloat16 [2, 65536, 896], P(None, ('rep', 'shard')), may hold values from -1.5 to 1.5
- old_master: float32 [4096, 896], P('shard'), may hold values from -1.5 to 1.5
- old_first: float32 [4096, 896], P('shard'), may hold values from -12 to 12
- old_second: float32 [4096, 896], P('shard'), may hold values from 1 to 50
- old_rows: int32 [4096], P('shard'), may hold values from 0 to 4095, as said below
Outputs:
- layer_out: bfloat16 [2, 65536, 896], P(None, ('rep', 'shard'))
- input_grad: bfloat16 [2, 65536, 4096], P(None, ('rep', 'shard'))
- new_master: float32 [4096, 896], P('shard')
- new_first: float32 [4096, 896], P('shard')
- new_second: float32 [4096, 896], P('shard')
The draws below stay inside these ranges and needn't reach their ends.
Inputs may be any that keep to these rules, and one draw needn't show every extreme that they name: `old_rows`: every weight row is named exactly once; the 64 entries of each aligned block name exactly 1 row of each aligned range of 64 rows.
All inputs are finite; a program needn't handle non-finite values.
Results may differ from the reference program's by a relative error of at most 0.0049.
Values may be sent and summed in bfloat16 or wider, within the bound.
No kernel may reach another device: no remote copies, remote signals or barrier semaphores. Data moves between devices by JAX's collectives and lax.ppermute only.
A program may use at most 128 MiB of HBM per device.

```python
import math
import jax
import jax.numpy as jnp
from jax import lax

D = 4096
FF = 896
MICRO = 2
TOK_MB = 65536
ROWS_DEV = 64
PER_PEER = 1


def draw_old_rows(key, part):
    key = jax.random.fold_in(key, 7)
    owners = D // ROWS_DEV
    owner_key, slot_key = jax.random.split(key)

    def owner_perm(position):
        return jax.random.permutation(jax.random.fold_in(owner_key, position), ROWS_DEV)

    def slot_perm(position):
        return jax.random.permutation(jax.random.fold_in(slot_key, position), ROWS_DEV)
    within = jax.vmap(owner_perm)(jnp.arange(owners))
    row_ids = within + (jnp.arange(owners) * ROWS_DEV)[:, None]
    row_ids = row_ids.reshape(owners, owners, PER_PEER).transpose(1, 0, 2).reshape(owners, ROWS_DEV)
    shuffle = jax.vmap(slot_perm)(jnp.arange(owners))
    return jnp.take_along_axis(row_ids, shuffle, axis=1).reshape(D).astype(jnp.int32)


def strengthened(values, own_key, source, target, parts, factor):
    owner, partner = [(jnp.arange(values.shape[axis_at]) // (values.shape[axis_at] // parts)).reshape([-1 if axis == axis_at else 1 for axis in range(values.ndim)]) for axis_at in (source, target)]
    chosen = jax.random.permutation(own_key, parts)[partner]
    strong = (owner == chosen) | (owner == (partner + parts // 2) % parts)
    return jnp.where(strong, factor * values, values)


def level_of(stream_key, dims, pieces, smallest, largest):
    def one(dim, blocks):
        steps = jax.random.uniform(jax.random.fold_in(jax.random.fold_in(stream_key, 6), dim), (blocks,), jnp.float32, smallest / len(pieces), largest / len(pieces))
        return jnp.repeat(jnp.exp(steps), dims[dim] // blocks).reshape((-1,) + (1,) * (len(dims) - dim - 1))

    gain = one(*pieces[0])
    for cut in pieces[1:]:
        gain = gain * one(*cut)
    return gain


def noise(stream_key, extent, spread, most, shards=(), held_as=jnp.bfloat16):
    level = level_of(stream_key, extent, shards, -0.22, 0.18) if shards else 1.0
    entries = jax.random.normal(stream_key, extent, jnp.float32) * spread * level
    return jnp.minimum(jnp.maximum(entries, -most), most).astype(held_as)


def noise_with(own_key, dims, deviation, bound, pieces, heavy, held_as=jnp.bfloat16):
    values = deviation * jax.random.normal(own_key, dims, jnp.float32)
    if pieces:
        values = values * level_of(own_key, dims, pieces, -0.22, 0.18)
    return jnp.clip(strengthened(values, jax.random.fold_in(own_key, 3), *heavy), -bound, bound).astype(held_as)


def setup_inputs(seed: int = 0) -> dict:
    seeds = jax.random.split(jax.random.key(seed), 7)
    return {
        "activations": noise_with(seeds[0], (MICRO, TOK_MB, D), 0.25, 6.0, ((1, 256),), (1, 2, 256, 6.0)),
        "output_grad": noise(seeds[1], (MICRO, TOK_MB, FF), 0.25, 1.5, ((1, 256),)),
        "old_master": noise(seeds[2], (D, FF), 0.25, 1.5, ((0, 64),), jnp.float32),
        "old_first": noise(seeds[3], (D, FF), 2.0, 12.0, ((0, 64),), jnp.float32),
        "old_second": jnp.clip(jnp.exp(math.log(50.0) - 3.912023 * jax.random.uniform(seeds[4], (D, FF), jnp.float32) ** level_of(seeds[4], (D, FF), ((0, 64),), -0.2, 0.2)), 1.0, 50.0),
        "old_rows": draw_old_rows(jax.random.fold_in(seeds[6], 71), 0),
    }


correct_one = 1.0 - math.exp(1001.0 * math.log(0.9))
correct_two = 1.0 - math.exp(1001.0 * math.log(0.95))

def adam_update(master, first, second, gradient):
    first_next = 0.9 * first + 0.1 * gradient
    second_next = 0.95 * second + 0.05 * gradient * gradient
    update = first_next / correct_one / (jnp.sqrt(second_next / correct_two) + 1e-08)
    master_next = master - 0.05 * (update + 0.1 * master)
    return (master_next, first_next, second_next)

def reference(activations, output_grad, old_master, old_first, old_second, old_rows):
    master = jnp.zeros_like(old_master).at[old_rows].set(old_master)
    first = jnp.zeros_like(old_first).at[old_rows].set(old_first)
    second = jnp.zeros_like(old_second).at[old_rows].set(old_second)
    weights = master.astype(jnp.bfloat16)
    block_rows = math.gcd(MICRO * TOK_MB, 4096)
    act_blocks = activations.reshape(-1, block_rows, D)
    grad_blocks = output_grad.reshape(-1, block_rows, FF)

    def accumulate(running, operands):
        act_block, grad_block = operands
        result = jnp.dot(act_block, weights, preferred_element_type=jnp.float32).astype(jnp.bfloat16)
        backward = jnp.dot(grad_block, weights.T, preferred_element_type=jnp.float32).astype(jnp.bfloat16)
        running = running + jnp.dot(act_block.T, grad_block, preferred_element_type=jnp.float32)
        return (running, (result, backward))
    gradient, (results, backwards) = lax.scan(accumulate, jnp.zeros((D, FF), jnp.float32), (act_blocks, grad_blocks))
    new_master, new_first, new_second = adam_update(master, first, second, gradient)
    layer_out = results.reshape(MICRO, TOK_MB, FF)
    input_grad = backwards.reshape(MICRO, TOK_MB, D)
    return (layer_out, input_grad, new_master, new_first, new_second)
```

```python
import math

import jax
import jax.numpy as jnp
from jax import lax
from jax.experimental import pallas as pl
from jax.experimental.pallas import tpu as pltpu
from jax.sharding import PartitionSpec as P

AXES = ("rep", "shard")
NX, NY, NZ = 4, 4, 8
ROWS, HID = 4096, 896
BF, F32 = jnp.bfloat16, jnp.float32
MIB = 1 << 20

correct_one = 1.0 - math.exp(1001.0 * math.log(0.9))
correct_two = 1.0 - math.exp(1001.0 * math.log(0.95))


def device_at(x, y, z, core):
    x, y, z, core = x % NX, y % NY, z % NZ, core % 2
    return ((x // 2) * 2 + core) * 64 + z * 8 + (x % 2) * 4 + y


def shifted(values, dx=0, dy=0, dz=0, dcore=0):
    pairs = [
        (device_at(x, y, z, c), device_at(x + dx, y + dy, z + dz, c + dcore))
        for x in range(NX)
        for y in range(NY)
        for z in range(NZ)
        for c in range(2)
    ]
    return lax.ppermute(values, AXES, pairs)


def position():
    rep, shard = lax.axis_index("rep"), lax.axis_index("shard")
    x = (rep // 2) * 2 + (shard // 4) % 2
    return jnp.stack([x, shard % 4, shard // 8, rep % 2]).astype(jnp.int32)


def call(body, pos, inputs, in_specs, outs, out_specs, grid=(1,), scratch=(), flops=0, vmem=48, aliases=None):
    moved = sum(a.size * a.dtype.itemsize for a in inputs)
    moved += sum(math.prod(s) * jnp.dtype(d).itemsize for s, d in outs)
    return pl.pallas_call(
        body,
        grid_spec=pltpu.PrefetchScalarGridSpec(
            num_scalar_prefetch=1,
            grid=grid,
            in_specs=in_specs,
            out_specs=out_specs,
            scratch_shapes=list(scratch),
        ),
        out_shape=[jax.ShapeDtypeStruct(s, d) for s, d in outs],
        input_output_aliases=aliases or {},
        compiler_params=pltpu.CompilerParams(vmem_limit_bytes=vmem * MIB),
        cost_estimate=pl.CostEstimate(flops=flops, bytes_accessed=moved, transcendentals=0),
    )(pos, *inputs)


def whole(shape):
    return pl.BlockSpec(shape, lambda i, pos: (0,) * len(shape))


def local_gradient(part, pos, acts, grads):
    def body(pos, acts_ref, grad_ref, send_ref, keep_ref, block):
        block[...] = lax.dot_general(
            acts_ref[...], grad_ref[...], (((0,), (0,)), ((), ())), preferred_element_type=F32
        )
        core = pos[3]
        for x in range(NX):
            for y in range(NY):
                base = (x % 2) * 256 + y * 64 + (x // 2) * 32
                at = (x, 0, y) if part == 0 else (y, 0, x)
                send_ref[at] = block[pl.ds(pl.multiple_of(base + (1 - core) * 16, 16), 16), :].astype(BF)
                keep_ref[at] = block[pl.ds(pl.multiple_of(base + core * 16, 16), 16), :]

    tokens = acts.shape[0]
    out = pl.BlockSpec((4, 1, 4, 16, HID), lambda i, pos: (0, i, 0, 0, 0))
    return call(
        body,
        pos,
        (acts, grads),
        [pl.BlockSpec((tokens, 512), lambda i, pos: (0, part * 4 + i)), whole((tokens, HID))],
        [((4, 4, 4, 16, HID), BF), ((4, 4, 4, 16, HID), F32)],
        [out, out],
        grid=(4,),
        scratch=[pltpu.VMEM((512, HID), F32)],
        flops=2 * tokens * 2048 * HID,
    )


def scatter_first(axis, pos, keep, got):
    def body(pos, keep_ref, got_ref, *outs):
        total = keep_ref[0] + got_ref[0].astype(F32)
        for step, out in enumerate(outs):

            @pl.when(pl.program_id(0) == step)
            def _():
                out[...] = total.astype(out.dtype)

    spec = pl.BlockSpec((1, 256, HID), lambda i, pos: ((pos[axis] + i) % 4, 0, 0))
    return call(
        body,
        pos,
        (keep.reshape(4, 256, HID), got.reshape(4, 256, HID)),
        [spec, spec],
        [((256, HID), F32)] + [((256, HID), BF)] * 3,
        [whole((256, HID))] * 4,
        grid=(4,),
    )


def scatter_second(axis, pos, own, got):
    def body(pos, own_ref, one, two, three, *outs):
        total = own_ref[...] + one[...].astype(F32) + two[...].astype(F32) + three[...].astype(F32)
        for step, out in enumerate(outs):

            @pl.when(pl.program_id(0) == step)
            def _():
                out[...] = total[:, 0].astype(out.dtype)

    spec = pl.BlockSpec((4, 1, 16, HID), lambda i, pos: (0, (pos[axis] + i) % 4, 0, 0))
    return call(
        body,
        pos,
        [a.reshape(4, 4, 16, HID) for a in (own, *got)],
        [spec] * 4,
        [((4, 16, HID), F32)] + [((4, 16, HID), BF)] * 3,
        [whole((4, 16, HID))] * 4,
        grid=(4,),
    )


def scatter_third(pos, parts):
    def body(pos, *refs):
        ins, outs, total = refs[:8], refs[8:16], refs[16]
        for part in range(2):
            own, one, two, three = ins[4 * part : 4 * part + 4]
            total[4 * part : 4 * part + 4] = (
                own[...] + one[...].astype(F32) + two[...].astype(F32) + three[...].astype(F32)
            )
        for step, out in enumerate(outs):
            out[...] = total[(pos[2] + step) % NZ].astype(out.dtype)

    return call(
        body,
        pos,
        parts,
        [whole((4, 16, HID))] * 8,
        [((16, HID), F32)] + [((16, HID), BF)] * 7,
        [whole((16, HID))] * 8,
        scratch=[pltpu.VMEM((NZ, 16, HID), F32)],
    )


def add_all(pos, own, got):
    def body(pos, *refs):
        total = refs[0][...]
        for ref in refs[1:-1]:
            total = total + ref[...].astype(F32)
        refs[-1][...] = total

    spec = whole((16, HID))
    return call(body, pos, (own, *got), [spec] * (1 + len(got)), [((16, HID), F32)], [spec])[0]


def adam(pos, pieces, master, first, second):
    def body(pos, g0, g1, g2, g3, m_ref, f_ref, s_ref, nm_ref, nf_ref, ns_ref, grad):
        rep = (pos[0] // 2) * 2 + pos[3]
        for flip, piece in enumerate((g0, g1, g2, g3)):
            grad[pl.ds(pl.multiple_of((rep ^ flip) * 16, 16), 16), :] = piece[...]
        gradient, master = grad[...], m_ref[...]
        first_next = 0.9 * f_ref[...] + 0.1 * gradient
        second_next = 0.95 * s_ref[...] + 0.05 * gradient * gradient
        update = first_next / correct_one / (jnp.sqrt(second_next / correct_two) + 1e-08)
        nm_ref[...] = master - 0.05 * (update + 0.1 * master)
        nf_ref[...] = first_next
        ns_ref[...] = second_next

    return call(
        body,
        pos,
        (*pieces, master, first, second),
        [whole((16, HID))] * 4 + [whole((64, HID))] * 3,
        [((64, HID), F32)] * 3,
        [whole((64, HID))] * 3,
        scratch=[pltpu.VMEM((64, HID), F32)],
    )


def place_weights(pos, arrived):
    def body(pos, in_ref, *outs):
        for which, out in enumerate(outs):
            at = which * 1024
            row = in_ref[:, at + HID : at + 1024].astype(F32)[:, :1]
            target = lax.broadcasted_iota(jnp.int32, (64, 64), 1).astype(F32)
            chosen = (row == target).astype(F32).astype(BF)
            out[...] = lax.dot_general(
                chosen, in_ref[:, at : at + HID], (((0,), (0,)), ((), ())), preferred_element_type=F32
            ).astype(BF)

    return call(
        body, pos, (arrived,), [whole((64, 2048))], [((64, HID), BF)] * 2, [whole((64, HID))] * 2
    )


def products(other, pos, acts, grads, blocks, carried=()):
    tokens = acts.shape[0]

    def body(pos, acts_ref, grad_ref, a_ref, b_ref, *refs):
        if other:
            acc_in, _, layer_ref, input_ref, weights, sems, acc = refs
        else:
            acc, input_ref, weights, sems = refs
        step = pl.program_id(0)

        @pl.when(step == 0)
        def _():
            copies = []
            for far in range(NX):
                for near in range(NY):
                    for which, ref in enumerate((a_ref, b_ref)):
                        dx, dy = (far, near) if which == 0 else (near, far)
                        x, y = (pos[0] + dx) % NX, (pos[1] + dy) % NY
                        row = (x // 2) * 1024 + which * 512 + (x % 2) * 256 + y * 64
                        copy = pltpu.make_async_copy(
                            ref.at[far * 4 + near],
                            weights.at[pl.ds(pl.multiple_of(row, 64), 64)],
                            sems.at[len(copies)],
                        )
                        copy.start()
                        copies.append(copy)
            for copy in copies:
                copy.wait()
            if other:
                acc[...] = acc_in[...]
            else:
                acc[...] = jnp.zeros_like(acc)

        rows = weights[pl.ds(pl.multiple_of(step * 512, 512), 512), :]
        acc[...] += jnp.dot(acts_ref[...], rows, preferred_element_type=F32)
        input_ref[...] = lax.dot_general(
            grad_ref[...], rows, (((1,), (1,)), ((), ())), preferred_element_type=F32
        ).astype(BF)
        if other:

            @pl.when(step == 3)
            def _():
                layer_ref[...] = acc[...].astype(BF)

    def column(i, pos):
        core = 1 - pos[3] if other else pos[3]
        return (0, 4 * (i // 2) + 2 * core + i % 2)

    piece = pl.BlockSpec((tokens, 512), column)
    anywhere = pl.BlockSpec(memory_space=pl.ANY)
    scratch = [pltpu.VMEM((2048, HID), BF), pltpu.SemaphoreType.DMA((32,))]
    inputs = [acts, grads] + [b.reshape(16, 64, HID) for b in blocks]
    in_specs = [piece, whole((tokens, HID)), anywhere, anywhere]
    if other:
        inputs += carried
        in_specs += [whole((tokens, HID)), anywhere]
        outs = [((tokens, HID), BF), ((tokens, ROWS), BF)]
        scratch.append(pltpu.VMEM((tokens, HID), F32))
    else:
        outs = [((tokens, HID), F32), ((tokens, ROWS), BF)]
    return call(
        body,
        pos,
        inputs,
        in_specs,
        outs,
        [whole((tokens, HID)), piece],
        grid=(4,),
        scratch=scratch,
        flops=4 * tokens * 2048 * HID,
        aliases={6: 1} if other else None,
    )


def per_device(activations, output_grad, old_master, old_first, old_second, old_rows):
    micro, tokens, width = activations.shape
    hidden = output_grad.shape[2]
    acts = activations.reshape(micro * tokens, width)
    grads = output_grad.reshape(micro * tokens, hidden)
    pos = position()
    rep = lax.axis_index("rep")
    owner, within = old_rows // 64, old_rows % 64

    lane = jnp.zeros((64, 128), BF) + within.astype(BF)[:, None]
    stored = jnp.concatenate([old_master.astype(BF), lane], axis=1)
    plane = jnp.arange(8)[:, None]
    wanted = ((2 * rep + jnp.arange(2)[None, :]) * 8 + plane).reshape(16)
    chosen = (wanted[:, None] == owner[None, :]).astype(BF)
    picked = jnp.dot(chosen, stored, preferred_element_type=F32).astype(BF).reshape(8, 2048)
    spread = jnp.broadcast_to(picked[None], (NZ, 8, 2048)).reshape(64, 2048)
    arrived = lax.all_to_all(spread, "shard", split_axis=0, concat_axis=0, tiled=True)
    part_a, part_b = place_weights(pos, arrived)

    sends, keeps = [], []
    for part in range(2):
        send, keep = local_gradient(part, pos, acts, grads)
        sends.append(shifted(send.reshape(1024, HID), dcore=1))
        keeps.append(keep)

    near_a = jnp.concatenate([part_a] + [shifted(part_a, dy=-d) for d in (1, 2, 3)])
    near_b = jnp.concatenate([part_b] + [shifted(part_b, dx=-d) for d in (1, 2, 3)])

    own_a, *far_a = scatter_first(0, pos, keeps[0], sends[0])
    far_a = [shifted(v, dx=d + 1) for d, v in enumerate(far_a)]
    own_b, *far_b = scatter_first(1, pos, keeps[1], sends[1])
    far_b = [shifted(v, dy=d + 1) for d, v in enumerate(far_b)]

    block_a = jnp.concatenate([near_a] + [shifted(near_a, dx=-d) for d in (1, 2, 3)])
    block_b = jnp.concatenate([near_b] + [shifted(near_b, dy=-d) for d in (1, 2, 3)])

    order = jnp.sum(jnp.where(owner[None, :] == jnp.arange(64)[:, None], jnp.arange(64)[None, :], 0), axis=1)
    marks = jnp.zeros((64, 128), F32) + within.astype(F32)[:, None]
    state = jnp.concatenate([old_master, old_first, old_second, marks], axis=1)[order]
    state = lax.all_to_all(state, "shard", split_axis=0, concat_axis=0, tiled=True)
    place = state[:, 3 * HID].astype(jnp.int32)
    source = jnp.sum(jnp.where(place[None, :] == jnp.arange(64)[:, None], jnp.arange(64)[None, :], 0), axis=1)
    state = state[source]
    master, first, second = (state[:, k * HID : (k + 1) * HID] for k in range(3))

    own_a, *near = scatter_second(1, pos, own_a, far_a)
    near = [shifted(v, dy=d + 1) for d, v in enumerate(near)]
    own_b, *near_too = scatter_second(0, pos, own_b, far_b)
    near_too = [shifted(v, dx=d + 1) for d, v in enumerate(near_too)]
    own, *along = scatter_third(pos, [own_a, *near, own_b, *near_too])
    along = [shifted(v, dz=d + 1) for d, v in enumerate(along)]
    total = add_all(pos, own, along)
    pieces = [total, shifted(total, dcore=1), shifted(total, dx=2), shifted(total, dx=2, dcore=1)]
    new_master, new_first, new_second = adam(pos, pieces, master, first, second)

    other_a, other_b = shifted(block_a, dcore=1), shifted(block_b, dcore=1)
    acc, half = products(False, pos, acts, grads, (block_a, block_b))
    layer_out, input_grad = products(True, pos, acts, grads, (other_a, other_b), (acc, half))
    return (
        layer_out.reshape(micro, tokens, hidden),
        input_grad.reshape(micro, tokens, width),
        new_master,
        new_first,
        new_second,
    )


def solution(mesh):
    in_specs = (
        P(None, AXES, None),
        P(None, AXES, None),
        P("shard", None),
        P("shard", None),
        P("shard", None),
        P("shard"),
    )
    out_specs = (
        P(None, AXES, None),
        P(None, AXES, None),
        P("shard", None),
        P("shard", None),
        P("shard", None),
    )
    return jax.shard_map(per_device, mesh=mesh, in_specs=in_specs, out_specs=out_specs, check_vma=False)
```

```python
import math

import jax
import jax.numpy as jnp
from jax import lax
from jax.experimental import pallas as pl
from jax.experimental.pallas import tpu as pltpu
from jax.sharding import PartitionSpec as P

AXES = ("rep", "shard")
NX, NY, NZ = 4, 4, 8
ROWS, HID = 4096, 896
BF, F32 = jnp.bfloat16, jnp.float32
MIB = 1 << 20
LONG = 200 * 10**9
SHRINK = 1000

correct_one = 1.0 - math.exp(1001.0 * math.log(0.9))
correct_two = 1.0 - math.exp(1001.0 * math.log(0.95))


def device_at(x, y, z, core):
    x, y, z, core = x % NX, y % NY, z % NZ, core % 2
    return ((x // 2) * 2 + core) * 64 + z * 8 + (x % 2) * 4 + y


def shifted(values, dx=0, dy=0, dz=0, dcore=0):
    pairs = [
        (device_at(x, y, z, c), device_at(x + dx, y + dy, z + dz, c + dcore))
        for x in range(NX)
        for y in range(NY)
        for z in range(NZ)
        for c in range(2)
    ]
    return lax.ppermute(values, AXES, pairs)


def position():
    rep, shard = lax.axis_index("rep"), lax.axis_index("shard")
    x = (rep // 2) * 2 + (shard // 4) % 2
    return jnp.stack([x, shard % 4, shard // 8, rep % 2]).astype(jnp.int32)


def call(body, pos, inputs, in_specs, outs, out_specs, grid=(1,), scratch=(), flops=0, vmem=12, aliases=None, after=(), far=False, long=0):
    moved = sum(a.size * a.dtype.itemsize for a in inputs)
    moved += sum(math.prod(s) * jnp.dtype(d).itemsize for s, d in outs)
    first, last = 1 + len(inputs), 1 + len(inputs) + len(after)

    def held_back(*refs):
        body(*refs[:first], *refs[last:])

    return pl.pallas_call(
        held_back,
        grid_spec=pltpu.PrefetchScalarGridSpec(
            num_scalar_prefetch=1,
            grid=grid,
            in_specs=list(in_specs) + [pl.BlockSpec(memory_space=pltpu.HBM)] * len(after),
            out_specs=out_specs,
            scratch_shapes=list(scratch),
        ),
        out_shape=[(pltpu.HBM if far and d != F32 else jax.ShapeDtypeStruct)(s, d) for s, d in outs],
        input_output_aliases=aliases or {},
        compiler_params=pltpu.CompilerParams(vmem_limit_bytes=vmem * MIB),
        cost_estimate=pl.CostEstimate(flops=long or flops // SHRINK, bytes_accessed=moved // SHRINK, transcendentals=0),
    )(pos, *inputs, *after)


def whole(shape):
    return pl.BlockSpec(shape, lambda i, pos: (0,) * len(shape))


def local_gradient(part, pos, acts, grads, got=None, after=()):
    def body(pos, acts_ref, grad_ref, *refs):
        block = lax.dot_general(
            acts_ref[...], grad_ref[...], (((0,), (0,)), ((), ())), preferred_element_type=F32
        )
        if got is None:
            for x in range(NX):
                for y in range(NY):
                    base = (x % 2) * 256 + y * 64 + (x // 2) * 32
                    at = (x, 0, y) if part == 0 else (y, 0, x)
                    refs[0][at] = block[base : base + 32].astype(BF)
            return
        got_ref, own, plus, minus, later_plus, later_minus, held = refs
        held[...] = block

        def write(out, step):
            to = (pos[part] + step) % 4
            for other in range(4):
                x, y = (to, other) if part == 0 else (other, to)
                base = (x % 2) * 256 + y * 64 + (x // 2) * 32
                rows = held[pl.ds(pl.multiple_of(base, 32), 32), :] + got_ref[to, 0, other].astype(F32)
                out[0, other] = rows.astype(out.dtype)

        write(own, 0)

        @pl.when(pl.program_id(0) == 0)
        def _():
            write(plus, 2)
            write(minus, 3)
            write(later_plus, 1)

        @pl.when(pl.program_id(0) == 1)
        def _():
            write(plus, 1)
            write(minus, 2)
            write(later_minus, 3)

    tokens = acts.shape[0]
    shape = (4, 2, 4, 32, HID)
    spec = pl.BlockSpec((4, 1, 4, 32, HID), lambda i, pos: (0, i, 0, 0, 0))

    def column(i, pos):
        core = 1 - pos[3] if got is None else pos[3]
        return (0, 2 * (2 * part + i) + core)

    ins = [pl.BlockSpec((tokens, 512), column), whole((tokens, HID))]
    flops = 2 * tokens * 1024 * HID
    if got is None:
        return call(body, pos, (acts, grads), ins, [(shape, BF)], [spec], grid=(2,), flops=flops, vmem=16, after=after)[0]
    out = pl.BlockSpec((1, 4, 32, HID), lambda i, pos: (i, 0, 0, 0))
    return call(
        body,
        pos,
        (acts, grads, got.reshape(shape)),
        ins + [spec],
        [((2, 4, 32, HID), F32)] + [((2, 4, 32, HID), BF)] * 2 + [((1, 4, 32, HID), F32)] * 2,
        [out] * 3 + [whole((1, 4, 32, HID))] * 2,
        grid=(2,),
        scratch=[pltpu.VMEM((512, HID), F32)],
        flops=flops,
        vmem=16,
        after=after,
        far=True,
    )


def ring(axis):
    groups = {}
    for x in range(NX):
        for y in range(NY):
            for z in range(NZ):
                for c in range(2):
                    at = {"x": x, "y": y, "z": z, "core": c}
                    key = tuple(v for k, v in at.items() if k != axis)
                    groups.setdefault(key, []).append(device_at(x, y, z, c))
    return [groups[k] for k in sorted(groups)]


def exchange(values, axis):
    return lax.all_to_all(
        values, AXES, split_axis=0, concat_axis=0, tiled=True, axis_index_groups=ring(axis)
    )


def gather(values, axis):
    return lax.all_gather(values, AXES, axis=0, tiled=True, axis_index_groups=ring(axis))


def add_opposite(pos, parts, after):
    def body(pos, *refs):
        ins, outs = refs[:8], refs[8:]
        for k in range(4):
            outs[k][...] = (ins[2 * k][...] + ins[2 * k + 1][...].astype(F32)).astype(BF)

    half = (1, 4, 32, HID)
    second_half = pl.BlockSpec(half, lambda i, pos: (1, 0, 0, 0))
    return call(
        body,
        pos,
        parts,
        [whole(half), whole(half), whole(half), second_half] * 2,
        [(half, BF)] * 4,
        [whole(half)] * 4,
        far=True,
        after=after,
    )


def sum_rings(pos, pieces_a, pieces_b, after):
    own_a, plus_a, minus_a, later_plus_a, later_minus_a = pieces_a
    own_b, plus_b, minus_b, later_plus_b, later_minus_b = pieces_b
    last_a, next_a = shifted(plus_a, dx=1), shifted(minus_a, dx=-1)
    last_b, next_b = shifted(plus_b, dy=1), shifted(minus_b, dy=-1)
    up_a, down_a, up_b, down_b = add_opposite(
        pos, (later_plus_a, last_a, later_minus_a, next_a, later_plus_b, last_b, later_minus_b, next_b), after
    )
    return (
        (own_a, last_a, next_a, shifted(up_a, dx=1), shifted(down_a, dx=-1)),
        (own_b, last_b, next_b, shifted(up_b, dy=1), shifted(down_b, dy=-1)),
    )


def add_first(pos, sum_a, sum_b, after):
    def body(pos, *refs):
        ins, outs = refs[:10], refs[10:]
        for part in range(2):
            own, last, following, both_last, both_next = ins[5 * part : 5 * part + 5]
            first = own[0, 0] + following[0, 0].astype(F32) + both_last[0, 0].astype(F32)
            second = own[1, 0] + last[0, 0].astype(F32) + both_next[0, 0].astype(F32)
            if part == 1:
                outs[4][0, 0] = first.astype(BF)
                outs[4][0, 1] = second.astype(BF)
                continue
            for step, out in enumerate(outs[:4]):

                @pl.when(pl.program_id(0) == step)
                def _():
                    out[0] = first.astype(out.dtype)
                    out[1] = second.astype(out.dtype)

    def spec(axis, size, at):
        return pl.BlockSpec((size, 1, 32, HID), lambda i, pos: (at, (pos[axis] + i) % 4, 0, 0))

    specs = []
    for axis in (1, 0):
        specs += [spec(axis, 2, 0), spec(axis, 1, 1), spec(axis, 1, 0), spec(axis, 1, 0), spec(axis, 1, 0)]
    return call(
        body,
        pos,
        (*sum_a, *sum_b),
        specs,
        [((2, 32, HID), F32)] + [((2, 32, HID), BF)] * 3 + [((4, 2, 32, HID), BF)],
        [whole((2, 32, HID))] * 4
        + [pl.BlockSpec((1, 2, 32, HID), lambda i, pos: ((pos[0] + i) % 4, 0, 0, 0))],
        grid=(4,),
        after=after,
        long=LONG,
    )


def add_second(pos, own_a, got_a, got_b):
    def body(pos, own, one, two, three, b_ref, out_ref):
        total = own[...] + one[...].astype(F32) + two[...].astype(F32) + three[...].astype(F32)
        out_ref[:4] = total.astype(BF)
        total = b_ref[0].astype(F32)
        for k in range(1, 4):
            total = total + b_ref[k].astype(F32)
        out_ref[4:] = total.astype(BF)

    shape = (4, 16, HID)
    return call(
        body,
        pos,
        [v.reshape(shape) for v in (own_a, *got_a)] + [got_b.reshape(4, *shape)],
        [whole(shape)] * 4 + [whole((4, *shape))],
        [((NZ, 16, HID), BF)],
        [whole((NZ, 16, HID))],
    )[0]


def add_third(pos, got, after):
    def body(pos, got_ref, out_ref):
        total = got_ref[0].astype(F32)
        for k in range(1, NZ):
            total = total + got_ref[k].astype(F32)
        out_ref[...] = total

    return call(
        body, pos, (got,), [whole((NZ, 16, HID))], [((16, HID), F32)], [whole((16, HID))], after=after
    )[0]


def to_owners(total):
    pieces = []
    for flip_x in range(2):
        for flip_z in range(2):
            pairs = []
            for x in range(NX):
                for y in range(NY):
                    for z in range(NZ):
                        for c in range(2):
                            source = device_at(x + 2 * flip_x, y, z - z % 2 + (c ^ flip_z), z % 2)
                            pairs.append((source, device_at(x, y, z, c)))
            pieces.append(lax.ppermute(total, AXES, pairs))
    return pieces


def permuted(chosen, values):
    high = values.astype(BF)
    rest = values - high.astype(F32)
    middle = rest.astype(BF)
    low = (rest - middle.astype(F32)).astype(BF)

    def times(term):
        return lax.dot_general(chosen, term, (((1,), (0,)), ((), ())), preferred_element_type=F32)

    return (times(high) + times(middle)) + times(low)


def outgoing(pos, rows, master, first, second, after):
    def body(pos, rows_ref, m_ref, f_ref, s_ref, weights_ref, state_ref, lines):
        rep = (pos[0] // 2) * 2 + pos[3]
        owner = lax.shift_right_logical(rows_ref[...], 6)
        within = jnp.bitwise_and(rows_ref[...], 63).astype(F32).astype(BF)
        within = jnp.broadcast_to(within, (128, 64))
        master = m_ref[...]

        def select(wanted, count):
            return (jnp.broadcast_to(owner, (count, 64)) == wanted).astype(F32).astype(BF)

        def mark(chosen):
            return lax.dot_general(chosen, within, (((1,), (1,)), ((), ())), preferred_element_type=F32)

        to = lax.broadcasted_iota(jnp.int32, (8, 64), 0)
        for k in range(8):
            if k < 4:
                wanted = 2 * rep * 8 + jnp.bitwise_and(to, 4) + k
            else:
                z, x_low = 2 * (((k - 4) // 2) * 2 + pos[3]) + 1, (k - 4) % 2
                wanted = z * 8 + x_low * 4 + jnp.bitwise_and(to, 3)
            chosen = select(wanted, 8)
            picked = jnp.dot(chosen, master.astype(BF), preferred_element_type=F32)
            for line in range(7):
                lines[pl.ds(k * 8 + line, 8, stride=64), :] = picked[:, line * 128 : line * 128 + 128]
            lines[pl.ds(k * 8 + 7, 8, stride=64), :] = mark(chosen)
        weights = lines[...].astype(BF)
        for z in range(NZ):
            weights_ref[z] = weights

        chosen = select(lax.broadcasted_iota(jnp.int32, (64, 64), 0), 64)
        for k, values in enumerate((master, f_ref[...], s_ref[...])):
            moved = permuted(chosen, values)
            for line in range(7):
                state_ref[pl.ds(k * 7 + line, 64, stride=24), :] = moved[:, line * 128 : line * 128 + 128]
        marks = mark(chosen)
        for line in range(21, 24):
            state_ref[pl.ds(line, 64, stride=24), :] = marks

    weights, state = call(
        body,
        pos,
        (rows.reshape(1, 64), master, first, second),
        [whole((1, 64))] + [whole((64, HID))] * 3,
        [((NZ, 512, 128), BF), ((64 * 24, 128), F32)],
        [whole((NZ, 512, 128)), whole((64 * 24, 128))],
        scratch=[pltpu.VMEM((512, 128), F32)],
        after=after,
    )
    return weights.reshape(64, 64, 128), state.reshape(64, 24, 128)


def held_until(pos, values, after):
    def body(pos, *refs):
        pass

    count = len(values)
    anywhere = pl.BlockSpec(memory_space=pltpu.HBM)
    return call(
        body,
        pos,
        values,
        [anywhere] * count,
        [(v.shape, v.dtype) for v in values],
        [anywhere] * count,
        vmem=1,
        aliases={1 + k: k for k in range(count)},
        after=after,
        far=True,
    )


def place_of(marks):
    target = lax.broadcasted_iota(jnp.int32, (64, 64), 1).astype(F32)
    return (marks[:, :64] == target).astype(F32).astype(BF)


def adam(pos, pieces, state, after):
    def body(pos, g0, g1, g2, g3, state_ref, nm_ref, nf_ref, ns_ref, grad):
        for which, piece in enumerate((g0, g1, g2, g3)):
            place = ((pos[0] // 2) ^ (which // 2)) * 32 + (pos[3] ^ (which % 2)) * 16
            grad[pl.ds(pl.multiple_of(place, 16), 16), :] = piece[...]
        chosen = place_of(state_ref[pl.ds(21, 64, stride=24), :]).T

        def arrived(k):
            lines = [state_ref[pl.ds(k * 7 + line, 64, stride=24), :] for line in range(7)]
            return permuted(chosen, jnp.concatenate(lines, axis=1))

        gradient, master = grad[...], arrived(0)
        first_next = 0.9 * arrived(1) + 0.1 * gradient
        second_next = 0.95 * arrived(2) + 0.05 * gradient * gradient
        update = first_next / correct_one / (jnp.sqrt(second_next / correct_two) + 1e-08)
        nm_ref[...] = master - 0.05 * (update + 0.1 * master)
        nf_ref[...] = first_next
        ns_ref[...] = second_next

    return call(
        body,
        pos,
        (*pieces, state.reshape(64 * 24, 128)),
        [whole((16, HID))] * 4 + [whole((64 * 24, 128))],
        [((64, HID), F32)] * 3,
        [whole((64, HID))] * 3,
        scratch=[pltpu.VMEM((64, HID), F32)],
        after=after,
    )


def place_weights(pos, arrived, after):
    def body(pos, in_ref, a_ref, b_ref, lines):
        lines[...] = in_ref[...].astype(F32)
        for k in range(8):
            chosen = place_of(lines[pl.ds(k * 8 + 7, 64, stride=64), :])
            rows = [lines[pl.ds(k * 8 + line, 64, stride=64), :] for line in range(7)]
            rows = jnp.concatenate(rows, axis=1).astype(BF)
            out = a_ref if k < 4 else b_ref
            out[(k % 4) * 64 : (k % 4) * 64 + 64] = lax.dot_general(
                chosen, rows, (((0,), (0,)), ((), ())), preferred_element_type=F32
            ).astype(BF)

    return call(
        body,
        pos,
        (arrived.reshape(4096, 128),),
        [whole((4096, 128))],
        [((256, HID), BF)] * 2,
        [whole((256, HID))] * 2,
        scratch=[pltpu.VMEM((4096, 128), F32)],
        after=after,
        long=LONG,
    )


def products(other, pos, acts, grads, blocks, carried=(), after=()):
    tokens = acts.shape[0]

    def body(pos, acts_ref, grad_ref, a_ref, b_ref, *refs):
        if other:
            acc_in, _, layer_ref, input_ref, token, weights, sems, acc = refs
        else:
            acc, input_ref, token, weights, sems = refs
        step = pl.program_id(0)
        token[...] = jnp.zeros_like(token)

        def pieces(block):
            copies = []
            for x_low in range(2):
                for y in range(NY):
                    x, which = (block // 2) * 2 + x_low, block % 2
                    at = x * 4 + y if which == 0 else lax.rem(y - pos[1] + NY, NY) * 4 + x
                    row = block * 512 + x_low * 256 + y * 64
                    copies.append(
                        pltpu.make_async_copy(
                            (a_ref, b_ref)[which].at[at],
                            weights.at[pl.ds(row, 64)],
                            sems.at[block * 8 + x_low * 4 + y],
                        )
                    )
            return copies

        @pl.when(step == 0)
        def _():
            for block in range(4):
                for copy in pieces(block):
                    copy.start()
            acc[...] = acc_in[...] if other else jnp.zeros_like(acc)

        for block in range(4):

            @pl.when(step == block)
            def _():
                for copy in pieces(block):
                    copy.wait()

        rows = weights[pl.ds(pl.multiple_of(step * 512, 512), 512), :]
        acc[...] += jnp.dot(acts_ref[...], rows, preferred_element_type=F32)
        input_ref[...] = lax.dot_general(
            grad_ref[...], rows, (((1,), (1,)), ((), ())), preferred_element_type=F32
        ).astype(BF)
        if other:

            @pl.when(step == 3)
            def _():
                layer_ref[...] = acc[...].astype(BF)

    def column(i, pos):
        core = 1 - pos[3] if other else pos[3]
        return (0, 4 * (i // 2) + 2 * core + i % 2)

    piece = pl.BlockSpec((tokens, 512), column)
    anywhere = pl.BlockSpec(memory_space=pltpu.HBM)
    scratch = [pltpu.VMEM((2048, HID), BF), pltpu.SemaphoreType.DMA((32,))]
    inputs = [acts, grads] + [b.reshape(16, 64, HID) for b in blocks]
    in_specs = [piece, whole((tokens, HID)), anywhere, anywhere]
    if other:
        inputs += carried
        in_specs += [whole((tokens, HID)), anywhere]
        outs = [((tokens, HID), BF), ((tokens, ROWS), BF)]
        scratch.append(pltpu.VMEM((tokens, HID), F32))
    else:
        outs = [((tokens, HID), F32), ((tokens, ROWS), BF)]
    return call(
        body,
        pos,
        inputs,
        in_specs,
        outs + [((8, 128), F32)],
        [whole((tokens, HID)), piece, whole((8, 128))],
        grid=(4,),
        scratch=scratch,
        flops=4 * tokens * 2048 * HID,
        vmem=56,
        after=after,
        aliases={6: 1} if other else None,
    )


def per_device(activations, output_grad, old_master, old_first, old_second, old_rows):
    micro, tokens, width = activations.shape
    hidden = output_grad.shape[2]
    acts = activations.reshape(micro * tokens, width)
    grads = output_grad.reshape(micro * tokens, hidden)
    pos = position()

    terms = [local_gradient(part, pos, acts, grads) for part in range(2)]
    got = [shifted(t.reshape(1024, HID), dcore=1) for t in terms]
    weights, state = outgoing(pos, old_rows, old_master, old_first, old_second, (terms[1],))
    arrived = lax.all_to_all(weights, "shard", split_axis=0, concat_axis=0, tiled=True)

    pieces_a = local_gradient(0, pos, acts, grads, got[0], after=(weights,))
    pieces_b = local_gradient(1, pos, acts, grads, got[1], after=(pieces_a[1],))
    part_a, part_b = place_weights(pos, arrived, after=(pieces_b[1],))
    sum_a, sum_b = sum_rings(pos, pieces_a, pieces_b, (part_a,))

    block_a = gather(held_until(pos, (part_a,), sum_a[3:])[0], "x")
    state = lax.all_to_all(state, "shard", split_axis=0, concat_axis=0, tiled=True)

    own_a, one, two, three, all_b = add_first(pos, sum_a, sum_b, (state,))
    got_a = [shifted(v, dy=d + 1) for d, v in enumerate((one, two, three))]
    part_b = held_until(pos, (part_b,), got_a)[0]
    block_b = jnp.concatenate([part_b] + [shifted(part_b, dy=-d) for d in (1, 2, 3)])
    second = add_second(pos, own_a, got_a, exchange(all_b, "x"))
    total = add_third(pos, exchange(second, "z"), ())
    owned = to_owners(total)

    block_a, block_b = held_until(pos, (block_a, block_b), (total,))
    other_a, other_b = shifted(block_a, dcore=1), shifted(block_b, dcore=1)
    acc, half, done = products(False, pos, acts, grads, (block_a, block_b))
    layer_out, input_grad, done = products(True, pos, acts, grads, (other_a, other_b), (acc, half))
    new_master, new_first, new_second = adam(pos, owned, state, (done,))
    return (
        layer_out.reshape(micro, tokens, hidden),
        input_grad.reshape(micro, tokens, width),
        new_master,
        new_first,
        new_second,
    )


def solution(mesh):
    in_specs = (
        P(None, AXES, None),
        P(None, AXES, None),
        P("shard", None),
        P("shard", None),
        P("shard", None),
        P("shard"),
    )
    out_specs = (
        P(None, AXES, None),
        P(None, AXES, None),
        P("shard", None),
        P("shard", None),
        P("shard", None),
    )
    return jax.shard_map(per_device, mesh=mesh, in_specs=in_specs, out_specs=out_specs, check_vma=False)
```

```python
import math

import jax
import jax.numpy as jnp
from jax import lax
from jax.experimental import pallas as pl
from jax.experimental.pallas import tpu as pltpu
from jax.sharding import PartitionSpec as P

AXES = ("rep", "shard")
NX, NY, NZ = 4, 4, 8
ROWS, HID = 4096, 896
BF, F32 = jnp.bfloat16, jnp.float32
MIB = 1 << 20
TOKEN = ((8, 128), F32)
LONG = 200 * 10**9
SHRINK = 1000

correct_one = 1.0 - math.exp(1001.0 * math.log(0.9))
correct_two = 1.0 - math.exp(1001.0 * math.log(0.95))


def device_at(x, y, z, core):
    x, y, z, core = x % NX, y % NY, z % NZ, core % 2
    return ((x // 2) * 2 + core) * 64 + z * 8 + (x % 2) * 4 + y


def shifted(values, dx=0, dy=0, dz=0, dcore=0):
    pairs = [
        (device_at(x, y, z, c), device_at(x + dx, y + dy, z + dz, c + dcore))
        for x in range(NX)
        for y in range(NY)
        for z in range(NZ)
        for c in range(2)
    ]
    return lax.ppermute(values, AXES, pairs)


def position():
    rep, shard = lax.axis_index("rep"), lax.axis_index("shard")
    x = (rep // 2) * 2 + (shard // 4) % 2
    return jnp.stack([x, shard % 4, shard // 8, rep % 2]).astype(jnp.int32)


def call(body, pos, inputs, in_specs, outs, out_specs, grid=(1,), scratch=(), flops=0, vmem=12, aliases=None, after=(), far=False, long=0):
    moved = sum(a.size * a.dtype.itemsize for a in inputs)
    moved += sum(math.prod(s) * jnp.dtype(d).itemsize for s, d in outs)
    first, last = 1 + len(inputs), 1 + len(inputs) + len(after)

    def held_back(*refs):
        body(*refs[:first], *refs[last:])

    return pl.pallas_call(
        held_back,
        grid_spec=pltpu.PrefetchScalarGridSpec(
            num_scalar_prefetch=1,
            grid=grid,
            in_specs=list(in_specs) + [pl.BlockSpec(memory_space=pl.ANY)] * len(after),
            out_specs=out_specs,
            scratch_shapes=list(scratch),
        ),
        out_shape=[(pltpu.HBM if far and d != F32 else jax.ShapeDtypeStruct)(s, d) for s, d in outs],
        input_output_aliases=aliases or {},
        compiler_params=pltpu.CompilerParams(vmem_limit_bytes=vmem * MIB),
        cost_estimate=pl.CostEstimate(flops=long or flops // SHRINK, bytes_accessed=moved // SHRINK, transcendentals=0),
    )(pos, *inputs, *after)


def whole(shape):
    return pl.BlockSpec(shape, lambda i, pos: (0,) * len(shape))


def local_gradient(part, pos, acts, grads, got=None, after=()):
    def body(pos, acts_ref, grad_ref, *refs):
        block = lax.dot_general(
            acts_ref[...], grad_ref[...], (((0,), (0,)), ((), ())), preferred_element_type=F32
        )
        if got is None:
            for x in range(NX):
                for y in range(NY):
                    base = (x % 2) * 256 + y * 64 + (x // 2) * 32
                    at = (x, 0, y) if part == 0 else (y, 0, x)
                    refs[0][at] = block[base : base + 32].astype(BF)
            return
        got_ref, own, plus, minus, later_plus, later_minus, token, held = refs
        held[...] = block
        token[...] = jnp.zeros_like(token)

        def write(out, step):
            to = (pos[part] + step) % 4
            for other in range(4):
                x, y = (to, other) if part == 0 else (other, to)
                base = (x % 2) * 256 + y * 64 + (x // 2) * 32
                rows = held[pl.ds(pl.multiple_of(base, 32), 32), :] + got_ref[to, 0, other].astype(F32)
                out[0, other] = rows.astype(out.dtype)

        write(own, 0)

        @pl.when(pl.program_id(0) == 0)
        def _():
            write(plus, 2)
            write(minus, 3)
            write(later_plus, 1)

        @pl.when(pl.program_id(0) == 1)
        def _():
            write(plus, 1)
            write(minus, 2)
            write(later_minus, 3)

    tokens = acts.shape[0]
    shape = (4, 2, 4, 32, HID)
    spec = pl.BlockSpec((4, 1, 4, 32, HID), lambda i, pos: (0, i, 0, 0, 0))

    def column(i, pos):
        core = 1 - pos[3] if got is None else pos[3]
        return (0, 2 * (2 * part + i) + core)

    ins = [pl.BlockSpec((tokens, 512), column), whole((tokens, HID))]
    flops = 2 * tokens * 1024 * HID
    if got is None:
        return call(body, pos, (acts, grads), ins, [(shape, BF)], [spec], grid=(2,), flops=flops, vmem=16, after=after)[0]
    out = pl.BlockSpec((1, 4, 32, HID), lambda i, pos: (i, 0, 0, 0))
    return call(
        body,
        pos,
        (acts, grads, got.reshape(shape)),
        ins + [spec],
        [((2, 4, 32, HID), F32)] + [((2, 4, 32, HID), BF)] * 2 + [((1, 4, 32, HID), F32)] * 2 + [TOKEN],
        [out] * 3 + [whole((1, 4, 32, HID))] * 2 + [whole((8, 128))],
        grid=(2,),
        scratch=[pltpu.VMEM((512, HID), F32)],
        flops=flops,
        vmem=16,
        after=after,
        far=True,
    )


def ring(axis):
    groups = {}
    for x in range(NX):
        for y in range(NY):
            for z in range(NZ):
                for c in range(2):
                    at = {"x": x, "y": y, "z": z, "core": c}
                    key = tuple(v for k, v in at.items() if k != axis)
                    groups.setdefault(key, []).append(device_at(x, y, z, c))
    return [groups[k] for k in sorted(groups)]


def exchange(values, axis):
    return lax.all_to_all(
        values, AXES, split_axis=0, concat_axis=0, tiled=True, axis_index_groups=ring(axis)
    )


def gather(values, axis):
    return lax.all_gather(values, AXES, axis=0, tiled=True, axis_index_groups=ring(axis))


def add_opposite(pos, parts, after):
    def body(pos, *refs):
        ins, outs = refs[:8], refs[8:]
        for k in range(4):
            outs[k][...] = (ins[2 * k][...] + ins[2 * k + 1][...].astype(F32)).astype(BF)

    half = (1, 4, 32, HID)
    second_half = pl.BlockSpec(half, lambda i, pos: (1, 0, 0, 0))
    return call(
        body,
        pos,
        parts,
        [whole(half), whole(half), whole(half), second_half] * 2,
        [(half, BF)] * 4,
        [whole(half)] * 4,
        far=True,
        after=after,
    )


def sum_rings(pos, pieces_a, pieces_b, after):
    own_a, plus_a, minus_a, later_plus_a, later_minus_a = pieces_a
    own_b, plus_b, minus_b, later_plus_b, later_minus_b = pieces_b
    last_a, next_a = shifted(plus_a, dx=1), shifted(minus_a, dx=-1)
    last_b, next_b = shifted(plus_b, dy=1), shifted(minus_b, dy=-1)
    up_a, down_a, up_b, down_b = add_opposite(
        pos, (later_plus_a, last_a, later_minus_a, next_a, later_plus_b, last_b, later_minus_b, next_b), after
    )
    return (
        (own_a, last_a, next_a, shifted(up_a, dx=1), shifted(down_a, dx=-1)),
        (own_b, last_b, next_b, shifted(up_b, dy=1), shifted(down_b, dy=-1)),
    )


def add_first(pos, sum_a, sum_b, after):
    def body(pos, *refs):
        ins, outs = refs[:10], refs[10:]
        for part in range(2):
            own, last, following, both_last, both_next = ins[5 * part : 5 * part + 5]
            first = own[0, 0] + following[0, 0].astype(F32) + both_last[0, 0].astype(F32)
            second = own[1, 0] + last[0, 0].astype(F32) + both_next[0, 0].astype(F32)
            if part == 1:
                outs[4][0, 0] = first.astype(BF)
                outs[4][0, 1] = second.astype(BF)
                continue
            for step, out in enumerate(outs[:4]):

                @pl.when(pl.program_id(0) == step)
                def _():
                    out[0] = first.astype(out.dtype)
                    out[1] = second.astype(out.dtype)

    def spec(axis, size, at):
        return pl.BlockSpec((size, 1, 32, HID), lambda i, pos: (at, (pos[axis] + i) % 4, 0, 0))

    specs = []
    for axis in (1, 0):
        specs += [spec(axis, 2, 0), spec(axis, 1, 1), spec(axis, 1, 0), spec(axis, 1, 0), spec(axis, 1, 0)]
    return call(
        body,
        pos,
        (*sum_a, *sum_b),
        specs,
        [((2, 32, HID), F32)] + [((2, 32, HID), BF)] * 3 + [((4, 2, 32, HID), BF)],
        [whole((2, 32, HID))] * 4
        + [pl.BlockSpec((1, 2, 32, HID), lambda i, pos: ((pos[0] + i) % 4, 0, 0, 0))],
        grid=(4,),
        after=after,
        long=LONG,
    )


def add_second(pos, own_a, got_a, got_b):
    def body(pos, own, one, two, three, b_ref, out_ref):
        total = own[...] + one[...].astype(F32) + two[...].astype(F32) + three[...].astype(F32)
        out_ref[:4] = total.astype(BF)
        total = b_ref[0].astype(F32)
        for k in range(1, 4):
            total = total + b_ref[k].astype(F32)
        out_ref[4:] = total.astype(BF)

    shape = (4, 16, HID)
    return call(
        body,
        pos,
        [v.reshape(shape) for v in (own_a, *got_a)] + [got_b.reshape(4, *shape)],
        [whole(shape)] * 4 + [whole((4, *shape))],
        [((NZ, 16, HID), BF)],
        [whole((NZ, 16, HID))],
    )[0]


def add_third(pos, got, after):
    def body(pos, got_ref, out_ref):
        total = got_ref[0].astype(F32)
        for k in range(1, NZ):
            total = total + got_ref[k].astype(F32)
        out_ref[...] = total

    return call(
        body, pos, (got,), [whole((NZ, 16, HID))], [((16, HID), F32)], [whole((16, HID))], after=after
    )[0]


def to_owners(total):
    pieces = []
    for flip_x in range(2):
        for flip_z in range(2):
            pairs = []
            for x in range(NX):
                for y in range(NY):
                    for z in range(NZ):
                        for c in range(2):
                            source = device_at(x + 2 * flip_x, y, z - z % 2 + (c ^ flip_z), z % 2)
                            pairs.append((source, device_at(x, y, z, c)))
            pieces.append(lax.ppermute(total, AXES, pairs))
    return pieces


def permuted(chosen, values):
    high = values.astype(BF)
    rest = values - high.astype(F32)
    middle = rest.astype(BF)
    low = (rest - middle.astype(F32)).astype(BF)

    def times(term):
        return lax.dot_general(chosen, term, (((1,), (0,)), ((), ())), preferred_element_type=F32)

    return (times(high) + times(middle)) + times(low)


def outgoing(pos, rows, master, first, second, after):
    def body(pos, rows_ref, m_ref, f_ref, s_ref, weights_ref, state_ref, lines):
        rep = (pos[0] // 2) * 2 + pos[3]
        owner = lax.shift_right_logical(rows_ref[...], 6)
        within = jnp.bitwise_and(rows_ref[...], 63).astype(F32).astype(BF)
        within = jnp.broadcast_to(within, (128, 64))
        master = m_ref[...]

        def select(wanted, count):
            return (jnp.broadcast_to(owner, (count, 64)) == wanted).astype(F32).astype(BF)

        def mark(chosen):
            return lax.dot_general(chosen, within, (((1,), (1,)), ((), ())), preferred_element_type=F32)

        to = lax.broadcasted_iota(jnp.int32, (8, 64), 0)
        for k in range(8):
            if k < 4:
                wanted = 2 * rep * 8 + jnp.bitwise_and(to, 4) + k
            else:
                z, x_low = 2 * (((k - 4) // 2) * 2 + pos[3]) + 1, (k - 4) % 2
                wanted = z * 8 + x_low * 4 + jnp.bitwise_and(to, 3)
            chosen = select(wanted, 8)
            picked = jnp.dot(chosen, master.astype(BF), preferred_element_type=F32)
            for line in range(7):
                lines[pl.ds(k * 8 + line, 8, stride=64), :] = picked[:, line * 128 : line * 128 + 128]
            lines[pl.ds(k * 8 + 7, 8, stride=64), :] = mark(chosen)
        weights = lines[...].astype(BF)
        for z in range(NZ):
            weights_ref[z] = weights

        chosen = select(lax.broadcasted_iota(jnp.int32, (64, 64), 0), 64)
        for k, values in enumerate((master, f_ref[...], s_ref[...])):
            moved = permuted(chosen, values)
            for line in range(7):
                state_ref[pl.ds(k * 7 + line, 64, stride=24), :] = moved[:, line * 128 : line * 128 + 128]
        marks = mark(chosen)
        for line in range(21, 24):
            state_ref[pl.ds(line, 64, stride=24), :] = marks

    weights, state = call(
        body,
        pos,
        (rows.reshape(1, 64), master, first, second),
        [whole((1, 64))] + [whole((64, HID))] * 3,
        [((NZ, 512, 128), BF), ((64 * 24, 128), F32)],
        [whole((NZ, 512, 128)), whole((64 * 24, 128))],
        scratch=[pltpu.VMEM((512, 128), F32)],
        after=after,
    )
    return weights.reshape(64, 64, 128), state.reshape(64, 24, 128)


def held_until(pos, values, after):
    def body(pos, *refs):
        pass

    count = len(values)
    anywhere = pl.BlockSpec(memory_space=pltpu.HBM)
    return call(
        body,
        pos,
        values,
        [anywhere] * count,
        [(v.shape, v.dtype) for v in values],
        [anywhere] * count,
        vmem=1,
        aliases={1 + k: k for k in range(count)},
        after=after,
        far=True,
    )


def place_of(marks):
    target = lax.broadcasted_iota(jnp.int32, (64, 64), 1).astype(F32)
    return (marks[:, :64] == target).astype(F32).astype(BF)


def adam(pos, pieces, state, after):
    def body(pos, g0, g1, g2, g3, state_ref, nm_ref, nf_ref, ns_ref, grad):
        for which, piece in enumerate((g0, g1, g2, g3)):
            place = ((pos[0] // 2) ^ (which // 2)) * 32 + (pos[3] ^ (which % 2)) * 16
            grad[pl.ds(pl.multiple_of(place, 16), 16), :] = piece[...]
        chosen = place_of(state_ref[pl.ds(21, 64, stride=24), :]).T

        def arrived(k):
            lines = [state_ref[pl.ds(k * 7 + line, 64, stride=24), :] for line in range(7)]
            return permuted(chosen, jnp.concatenate(lines, axis=1))

        gradient, master = grad[...], arrived(0)
        first_next = 0.9 * arrived(1) + 0.1 * gradient
        second_next = 0.95 * arrived(2) + 0.05 * gradient * gradient
        update = first_next / correct_one / (jnp.sqrt(second_next / correct_two) + 1e-08)
        nm_ref[...] = master - 0.05 * (update + 0.1 * master)
        nf_ref[...] = first_next
        ns_ref[...] = second_next

    return call(
        body,
        pos,
        (*pieces, state.reshape(64 * 24, 128)),
        [whole((16, HID))] * 4 + [whole((64 * 24, 128))],
        [((64, HID), F32)] * 3,
        [whole((64, HID))] * 3,
        scratch=[pltpu.VMEM((64, HID), F32)],
        after=after,
    )


def place_weights(pos, arrived, after):
    def body(pos, in_ref, a_ref, b_ref, token, lines):
        token[...] = jnp.zeros_like(token)
        lines[...] = in_ref[...].astype(F32)
        for k in range(8):
            chosen = place_of(lines[pl.ds(k * 8 + 7, 64, stride=64), :])
            rows = [lines[pl.ds(k * 8 + line, 64, stride=64), :] for line in range(7)]
            rows = jnp.concatenate(rows, axis=1).astype(BF)
            out = a_ref if k < 4 else b_ref
            out[(k % 4) * 64 : (k % 4) * 64 + 64] = lax.dot_general(
                chosen, rows, (((0,), (0,)), ((), ())), preferred_element_type=F32
            ).astype(BF)

    return call(
        body,
        pos,
        (arrived.reshape(4096, 128),),
        [whole((4096, 128))],
        [((256, HID), BF)] * 2 + [TOKEN],
        [whole((256, HID))] * 2 + [whole((8, 128))],
        scratch=[pltpu.VMEM((4096, 128), F32)],
        after=after,
        far=True,
        long=LONG,
    )


def products(other, pos, acts, grads, blocks, carried=(), after=()):
    tokens = acts.shape[0]

    def body(pos, acts_ref, grad_ref, a_ref, b_ref, *refs):
        if other:
            acc_in, _, layer_ref, input_ref, token, weights, sems, acc = refs
        else:
            acc, input_ref, token, weights, sems = refs
        step = pl.program_id(0)
        token[...] = jnp.zeros_like(token)

        def pieces(block):
            copies = []
            for x_low in range(2):
                for y in range(NY):
                    x, which = (block // 2) * 2 + x_low, block % 2
                    at = x * 4 + y if which == 0 else lax.rem(y - pos[1] + NY, NY) * 4 + x
                    row = block * 512 + x_low * 256 + y * 64
                    copies.append(
                        pltpu.make_async_copy(
                            (a_ref, b_ref)[which].at[at],
                            weights.at[pl.ds(row, 64)],
                            sems.at[block * 8 + x_low * 4 + y],
                        )
                    )
            return copies

        @pl.when(step == 0)
        def _():
            for block in range(4):
                for copy in pieces(block):
                    copy.start()
            acc[...] = acc_in[...] if other else jnp.zeros_like(acc)

        for block in range(4):

            @pl.when(step == block)
            def _():
                for copy in pieces(block):
                    copy.wait()

        rows = weights[pl.ds(pl.multiple_of(step * 512, 512), 512), :]
        acc[...] += jnp.dot(acts_ref[...], rows, preferred_element_type=F32)
        input_ref[...] = lax.dot_general(
            grad_ref[...], rows, (((1,), (1,)), ((), ())), preferred_element_type=F32
        ).astype(BF)
        if other:

            @pl.when(step == 3)
            def _():
                layer_ref[...] = acc[...].astype(BF)

    def column(i, pos):
        core = 1 - pos[3] if other else pos[3]
        return (0, 4 * (i // 2) + 2 * core + i % 2)

    piece = pl.BlockSpec((tokens, 512), column)
    anywhere = pl.BlockSpec(memory_space=pltpu.HBM)
    scratch = [pltpu.VMEM((2048, HID), BF), pltpu.SemaphoreType.DMA((32,))]
    inputs = [acts, grads] + [b.reshape(16, 64, HID) for b in blocks]
    in_specs = [piece, whole((tokens, HID)), anywhere, anywhere]
    if other:
        inputs += carried
        in_specs += [whole((tokens, HID)), anywhere]
        outs = [((tokens, HID), BF), ((tokens, ROWS), BF)]
        scratch.append(pltpu.VMEM((tokens, HID), F32))
    else:
        outs = [((tokens, HID), F32), ((tokens, ROWS), BF)]
    return call(
        body,
        pos,
        inputs,
        in_specs,
        outs + [TOKEN],
        [whole((tokens, HID)), piece, whole((8, 128))],
        grid=(4,),
        scratch=scratch,
        flops=4 * tokens * 2048 * HID,
        vmem=56,
        after=after,
        aliases={6: 1} if other else None,
    )


def per_device(activations, output_grad, old_master, old_first, old_second, old_rows):
    micro, tokens, width = activations.shape
    hidden = output_grad.shape[2]
    acts = activations.reshape(micro * tokens, width)
    grads = output_grad.reshape(micro * tokens, hidden)
    pos = position()

    terms = [local_gradient(part, pos, acts, grads) for part in range(2)]
    got = [shifted(t.reshape(1024, HID), dcore=1) for t in terms]
    weights, state = outgoing(pos, old_rows, old_master, old_first, old_second, (terms[1],))
    arrived = lax.all_to_all(weights, "shard", split_axis=0, concat_axis=0, tiled=True)

    *pieces_a, done = local_gradient(0, pos, acts, grads, got[0], after=(weights,))
    *pieces_b, done = local_gradient(1, pos, acts, grads, got[1], after=(done,))
    part_a, part_b, done = place_weights(pos, arrived, after=(done,))
    sum_a, sum_b = sum_rings(pos, pieces_a, pieces_b, (done,))

    block_a = gather(held_until(pos, (part_a,), sum_a[3:])[0], "x")
    state = lax.all_to_all(state, "shard", split_axis=0, concat_axis=0, tiled=True)

    own_a, one, two, three, all_b = add_first(pos, sum_a, sum_b, (state,))
    got_a = [shifted(v, dy=d + 1) for d, v in enumerate((one, two, three))]
    part_b = held_until(pos, (part_b,), got_a)[0]
    block_b = jnp.concatenate([part_b] + [shifted(part_b, dy=-d) for d in (1, 2, 3)])
    second = add_second(pos, own_a, got_a, exchange(all_b, "x"))
    total = add_third(pos, exchange(second, "z"), ())
    owned = to_owners(total)

    block_a, block_b = held_until(pos, (block_a, block_b), (total,))
    other_a, other_b = shifted(block_a, dcore=1), shifted(block_b, dcore=1)
    acc, half, done = products(False, pos, acts, grads, (block_a, block_b))
    layer_out, input_grad, done = products(True, pos, acts, grads, (other_a, other_b), (acc, half))
    new_master, new_first, new_second = adam(pos, owned, state, (done,))
    return (
        layer_out.reshape(micro, tokens, hidden),
        input_grad.reshape(micro, tokens, width),
        new_master,
        new_first,
        new_second,
    )


def solution(mesh):
    in_specs = (
        P(None, AXES, None),
        P(None, AXES, None),
        P("shard", None),
        P("shard", None),
        P("shard", None),
        P("shard"),
    )
    out_specs = (
        P(None, AXES, None),
        P(None, AXES, None),
        P("shard", None),
        P("shard", None),
        P("shard", None),
    )
    return jax.shard_map(per_device, mesh=mesh, in_specs=in_specs, out_specs=out_specs, check_vma=False)
```

```python
import math

import jax
import jax.numpy as jnp
from jax import lax
from jax.experimental import pallas as pl
from jax.experimental.pallas import tpu as pltpu
from jax.sharding import PartitionSpec as P

AXES = ("rep", "shard")
NX, NY, NZ = 4, 4, 8
ROWS, HID = 4096, 896
BF, F32 = jnp.bfloat16, jnp.float32
MIB = 1 << 20
TOKEN = ((8, 128), F32)
LONG = 200 * 10**9
SHRINK = 1000

correct_one = 1.0 - math.exp(1001.0 * math.log(0.9))
correct_two = 1.0 - math.exp(1001.0 * math.log(0.95))


def device_at(x, y, z, core):
    x, y, z, core = x % NX, y % NY, z % NZ, core % 2
    return ((x // 2) * 2 + core) * 64 + z * 8 + (x % 2) * 4 + y


def shifted(values, dx=0, dy=0, dz=0, dcore=0):
    pairs = [
        (device_at(x, y, z, c), device_at(x + dx, y + dy, z + dz, c + dcore))
        for x in range(NX)
        for y in range(NY)
        for z in range(NZ)
        for c in range(2)
    ]
    return lax.ppermute(values, AXES, pairs)


def position():
    rep, shard = lax.axis_index("rep"), lax.axis_index("shard")
    x = (rep // 2) * 2 + (shard // 4) % 2
    return jnp.stack([x, shard % 4, shard // 8, rep % 2]).astype(jnp.int32)


def call(body, pos, inputs, in_specs, outs, out_specs, grid=(1,), scratch=(), flops=0, vmem=12, aliases=None, after=(), far=False, long=0):
    moved = sum(a.size * a.dtype.itemsize for a in inputs)
    moved += sum(math.prod(s) * jnp.dtype(d).itemsize for s, d in outs)
    first, last = 1 + len(inputs), 1 + len(inputs) + len(after)

    def held_back(*refs):
        body(*refs[:first], *refs[last:])

    return pl.pallas_call(
        held_back,
        grid_spec=pltpu.PrefetchScalarGridSpec(
            num_scalar_prefetch=1,
            grid=grid,
            in_specs=list(in_specs) + [pl.BlockSpec(memory_space=pl.ANY)] * len(after),
            out_specs=out_specs,
            scratch_shapes=list(scratch),
        ),
        out_shape=[(pltpu.HBM if far and d != F32 else jax.ShapeDtypeStruct)(s, d) for s, d in outs],
        input_output_aliases=aliases or {},
        compiler_params=pltpu.CompilerParams(vmem_limit_bytes=vmem * MIB),
        cost_estimate=pl.CostEstimate(flops=long or flops // SHRINK, bytes_accessed=moved // SHRINK, transcendentals=0),
    )(pos, *inputs, *after)


def whole(shape):
    return pl.BlockSpec(shape, lambda i, pos: (0,) * len(shape))


def local_gradient(part, pos, acts, grads, got=None, after=()):
    def body(pos, acts_ref, grad_ref, *refs):
        block = lax.dot_general(
            acts_ref[...], grad_ref[...], (((0,), (0,)), ((), ())), preferred_element_type=F32
        )
        if got is None:
            for x in range(NX):
                for y in range(NY):
                    base = (x % 2) * 256 + y * 64 + (x // 2) * 32
                    at = (x, 0, y) if part == 0 else (y, 0, x)
                    refs[0][at] = block[base : base + 32].astype(BF)
            return
        got_ref, own, plus, minus, later_plus, later_minus, token, held = refs
        held[...] = block
        token[...] = jnp.zeros_like(token)

        def write(out, step):
            to = (pos[part] + step) % 4
            for other in range(4):
                x, y = (to, other) if part == 0 else (other, to)
                base = (x % 2) * 256 + y * 64 + (x // 2) * 32
                rows = held[pl.ds(pl.multiple_of(base, 32), 32), :] + got_ref[to, 0, other].astype(F32)
                out[0, other] = rows.astype(out.dtype)

        write(own, 0)

        @pl.when(pl.program_id(0) == 0)
        def _():
            write(plus, 2)
            write(minus, 3)
            write(later_plus, 1)

        @pl.when(pl.program_id(0) == 1)
        def _():
            write(plus, 1)
            write(minus, 2)
            write(later_minus, 3)

    tokens = acts.shape[0]
    shape = (4, 2, 4, 32, HID)
    spec = pl.BlockSpec((4, 1, 4, 32, HID), lambda i, pos: (0, i, 0, 0, 0))

    def column(i, pos):
        core = 1 - pos[3] if got is None else pos[3]
        return (0, 2 * (2 * part + i) + core)

    ins = [pl.BlockSpec((tokens, 512), column), whole((tokens, HID))]
    flops = 2 * tokens * 1024 * HID
    if got is None:
        return call(body, pos, (acts, grads), ins, [(shape, BF)], [spec], grid=(2,), flops=flops, vmem=16, after=after)[0]
    out = pl.BlockSpec((1, 4, 32, HID), lambda i, pos: (i, 0, 0, 0))
    return call(
        body,
        pos,
        (acts, grads, got.reshape(shape)),
        ins + [spec],
        [((2, 4, 32, HID), F32)] + [((2, 4, 32, HID), BF)] * 2 + [((1, 4, 32, HID), F32)] * 2 + [TOKEN],
        [out] * 3 + [whole((1, 4, 32, HID))] * 2 + [whole((8, 128))],
        grid=(2,),
        scratch=[pltpu.VMEM((512, HID), F32)],
        flops=flops,
        vmem=16,
        after=after,
        far=True,
    )


def ring(axis):
    groups = {}
    for x in range(NX):
        for y in range(NY):
            for z in range(NZ):
                for c in range(2):
                    at = {"x": x, "y": y, "z": z, "core": c}
                    key = tuple(v for k, v in at.items() if k != axis)
                    groups.setdefault(key, []).append(device_at(x, y, z, c))
    return [groups[k] for k in sorted(groups)]


def exchange(values, axis):
    return lax.all_to_all(
        values, AXES, split_axis=0, concat_axis=0, tiled=True, axis_index_groups=ring(axis)
    )


def gather(values, axis):
    return lax.all_gather(values, AXES, axis=0, tiled=True, axis_index_groups=ring(axis))


def add_opposite(pos, parts, after):
    def body(pos, *refs):
        ins, outs = refs[:8], refs[8:]
        for k in range(4):
            outs[k][...] = (ins[2 * k][...] + ins[2 * k + 1][...].astype(F32)).astype(BF)

    half = (1, 4, 32, HID)
    second_half = pl.BlockSpec(half, lambda i, pos: (1, 0, 0, 0))
    return call(
        body,
        pos,
        parts,
        [whole(half), whole(half), whole(half), second_half] * 2,
        [(half, BF)] * 4,
        [whole(half)] * 4,
        far=True,
        after=after,
    )


def sum_rings(pos, pieces_a, pieces_b, after):
    own_a, plus_a, minus_a, later_plus_a, later_minus_a = pieces_a
    own_b, plus_b, minus_b, later_plus_b, later_minus_b = pieces_b
    last_a, next_a = shifted(plus_a, dx=1), shifted(minus_a, dx=-1)
    last_b, next_b = shifted(plus_b, dy=1), shifted(minus_b, dy=-1)
    up_a, down_a, up_b, down_b = add_opposite(
        pos, (later_plus_a, last_a, later_minus_a, next_a, later_plus_b, last_b, later_minus_b, next_b), after
    )
    return (
        (own_a, last_a, next_a, shifted(up_a, dx=1), shifted(down_a, dx=-1)),
        (own_b, last_b, next_b, shifted(up_b, dy=1), shifted(down_b, dy=-1)),
    )


def add_first(pos, sum_a, sum_b, after):
    def body(pos, *refs):
        ins, outs = refs[:10], refs[10:]
        for part in range(2):
            own, last, following, both_last, both_next = ins[5 * part : 5 * part + 5]
            first = own[0, 0] + following[0, 0].astype(F32) + both_last[0, 0].astype(F32)
            second = own[1, 0] + last[0, 0].astype(F32) + both_next[0, 0].astype(F32)
            if part == 1:
                outs[4][0, 0] = first.astype(BF)
                outs[4][0, 1] = second.astype(BF)
                continue
            for step, out in enumerate(outs[:4]):

                @pl.when(pl.program_id(0) == step)
                def _():
                    out[0] = first.astype(out.dtype)
                    out[1] = second.astype(out.dtype)

    def spec(axis, size, at):
        return pl.BlockSpec((size, 1, 32, HID), lambda i, pos: (at, (pos[axis] + i) % 4, 0, 0))

    specs = []
    for axis in (1, 0):
        specs += [spec(axis, 2, 0), spec(axis, 1, 1), spec(axis, 1, 0), spec(axis, 1, 0), spec(axis, 1, 0)]
    return call(
        body,
        pos,
        (*sum_a, *sum_b),
        specs,
        [((2, 32, HID), F32)] + [((2, 32, HID), BF)] * 3 + [((4, 2, 32, HID), BF)],
        [whole((2, 32, HID))] * 4
        + [pl.BlockSpec((1, 2, 32, HID), lambda i, pos: ((pos[0] + i) % 4, 0, 0, 0))],
        grid=(4,),
        after=after,
        long=LONG,
    )


def add_second(pos, own_a, got_a, got_b):
    def body(pos, own, one, two, three, b_ref, out_ref):
        total = own[...] + one[...].astype(F32) + two[...].astype(F32) + three[...].astype(F32)
        out_ref[:4] = total.astype(BF)
        total = b_ref[0].astype(F32)
        for k in range(1, 4):
            total = total + b_ref[k].astype(F32)
        out_ref[4:] = total.astype(BF)

    shape = (4, 16, HID)
    return call(
        body,
        pos,
        [v.reshape(shape) for v in (own_a, *got_a)] + [got_b.reshape(4, *shape)],
        [whole(shape)] * 4 + [whole((4, *shape))],
        [((NZ, 16, HID), BF)],
        [whole((NZ, 16, HID))],
    )[0]


def add_third(pos, got, after):
    def body(pos, got_ref, out_ref):
        total = got_ref[0].astype(F32)
        for k in range(1, NZ):
            total = total + got_ref[k].astype(F32)
        out_ref[...] = total

    return call(
        body, pos, (got,), [whole((NZ, 16, HID))], [((16, HID), F32)], [whole((16, HID))], after=after
    )[0]


def to_owners(total):
    pieces = []
    for flip_x in range(2):
        for flip_z in range(2):
            pairs = []
            for x in range(NX):
                for y in range(NY):
                    for z in range(NZ):
                        for c in range(2):
                            source = device_at(x + 2 * flip_x, y, z - z % 2 + (c ^ flip_z), z % 2)
                            pairs.append((source, device_at(x, y, z, c)))
            pieces.append(lax.ppermute(total, AXES, pairs))
    return pieces


def permuted(chosen, values):
    high = values.astype(BF)
    rest = values - high.astype(F32)
    middle = rest.astype(BF)
    low = (rest - middle.astype(F32)).astype(BF)

    def times(term):
        return lax.dot_general(chosen, term, (((1,), (0,)), ((), ())), preferred_element_type=F32)

    return (times(high) + times(middle)) + times(low)


def outgoing(pos, rows, master, first, second, after):
    def body(pos, rows_ref, m_ref, f_ref, s_ref, weights_ref, state_ref, token, lines):
        token[...] = jnp.zeros_like(token)
        rep = (pos[0] // 2) * 2 + pos[3]
        owner = lax.shift_right_logical(rows_ref[...], 6)
        within = jnp.bitwise_and(rows_ref[...], 63).astype(F32).astype(BF)
        within = jnp.broadcast_to(within, (128, 64))
        master = m_ref[...]

        def select(wanted, count):
            return (jnp.broadcast_to(owner, (count, 64)) == wanted).astype(F32).astype(BF)

        def mark(chosen):
            return lax.dot_general(chosen, within, (((1,), (1,)), ((), ())), preferred_element_type=F32)

        to = lax.broadcasted_iota(jnp.int32, (8, 64), 0)
        for k in range(8):
            if k < 4:
                wanted = 2 * rep * 8 + jnp.bitwise_and(to, 4) + k
            else:
                z, x_low = 2 * (((k - 4) // 2) * 2 + pos[3]) + 1, (k - 4) % 2
                wanted = z * 8 + x_low * 4 + jnp.bitwise_and(to, 3)
            chosen = select(wanted, 8)
            picked = jnp.dot(chosen, master.astype(BF), preferred_element_type=F32)
            for line in range(7):
                lines[pl.ds(k * 8 + line, 8, stride=64), :] = picked[:, line * 128 : line * 128 + 128]
            lines[pl.ds(k * 8 + 7, 8, stride=64), :] = mark(chosen)
        weights = lines[...].astype(BF)
        for z in range(NZ):
            weights_ref[z] = weights

        chosen = select(lax.broadcasted_iota(jnp.int32, (64, 64), 0), 64)
        for k, values in enumerate((master, f_ref[...], s_ref[...])):
            moved = permuted(chosen, values)
            for line in range(7):
                state_ref[pl.ds(k * 7 + line, 64, stride=24), :] = moved[:, line * 128 : line * 128 + 128]
        marks = mark(chosen)
        for line in range(21, 24):
            state_ref[pl.ds(line, 64, stride=24), :] = marks

    weights, state, token = call(
        body,
        pos,
        (rows.reshape(1, 64), master, first, second),
        [whole((1, 64))] + [whole((64, HID))] * 3,
        [((NZ, 512, 128), BF), ((64 * 24, 128), F32), TOKEN],
        [whole((NZ, 512, 128)), whole((64 * 24, 128)), whole((8, 128))],
        scratch=[pltpu.VMEM((512, 128), F32)],
        after=after,
        far=True,
    )
    return weights.reshape(64, 64, 128), state.reshape(64, 24, 128), token


def held_until(pos, values, after):
    def body(pos, *refs):
        pass

    count = len(values)
    anywhere = pl.BlockSpec(memory_space=pltpu.HBM)
    return call(
        body,
        pos,
        values,
        [anywhere] * count,
        [(v.shape, v.dtype) for v in values],
        [anywhere] * count,
        vmem=1,
        aliases={1 + k: k for k in range(count)},
        after=after,
        far=True,
    )


def place_of(marks):
    target = lax.broadcasted_iota(jnp.int32, (64, 64), 1).astype(F32)
    return (marks[:, :64] == target).astype(F32).astype(BF)


def adam(pos, pieces, state, after):
    def body(pos, g0, g1, g2, g3, state_ref, nm_ref, nf_ref, ns_ref, grad):
        for which, piece in enumerate((g0, g1, g2, g3)):
            place = ((pos[0] // 2) ^ (which // 2)) * 32 + (pos[3] ^ (which % 2)) * 16
            grad[pl.ds(pl.multiple_of(place, 16), 16), :] = piece[...]
        chosen = place_of(state_ref[pl.ds(21, 64, stride=24), :]).T

        def arrived(k):
            lines = [state_ref[pl.ds(k * 7 + line, 64, stride=24), :] for line in range(7)]
            return permuted(chosen, jnp.concatenate(lines, axis=1))

        gradient, master = grad[...], arrived(0)
        first_next = 0.9 * arrived(1) + 0.1 * gradient
        second_next = 0.95 * arrived(2) + 0.05 * gradient * gradient
        update = first_next / correct_one / (jnp.sqrt(second_next / correct_two) + 1e-08)
        nm_ref[...] = master - 0.05 * (update + 0.1 * master)
        nf_ref[...] = first_next
        ns_ref[...] = second_next

    return call(
        body,
        pos,
        (*pieces, state.reshape(64 * 24, 128)),
        [whole((16, HID))] * 4 + [whole((64 * 24, 128))],
        [((64, HID), F32)] * 3,
        [whole((64, HID))] * 3,
        scratch=[pltpu.VMEM((64, HID), F32)],
        after=after,
    )


def place_weights(pos, arrived, after):
    def body(pos, in_ref, a_ref, b_ref, token, lines):
        token[...] = jnp.zeros_like(token)
        lines[...] = in_ref[...].astype(F32)
        for k in range(8):
            chosen = place_of(lines[pl.ds(k * 8 + 7, 64, stride=64), :])
            rows = [lines[pl.ds(k * 8 + line, 64, stride=64), :] for line in range(7)]
            rows = jnp.concatenate(rows, axis=1).astype(BF)
            out = a_ref if k < 4 else b_ref
            out[(k % 4) * 64 : (k % 4) * 64 + 64] = lax.dot_general(
                chosen, rows, (((0,), (0,)), ((), ())), preferred_element_type=F32
            ).astype(BF)

    return call(
        body,
        pos,
        (arrived.reshape(4096, 128),),
        [whole((4096, 128))],
        [((256, HID), BF)] * 2 + [TOKEN],
        [whole((256, HID))] * 2 + [whole((8, 128))],
        scratch=[pltpu.VMEM((4096, 128), F32)],
        after=after,
        far=True,
        long=LONG,
    )


def products(other, pos, acts, grads, blocks, carried=(), after=()):
    tokens = acts.shape[0]

    def body(pos, acts_ref, grad_ref, a_ref, b_ref, *refs):
        if other:
            acc_in, _, layer_ref, input_ref, token, weights, sems, acc = refs
        else:
            acc, input_ref, token, weights, sems = refs
        step = pl.program_id(0)
        token[...] = jnp.zeros_like(token)

        def pieces(block):
            copies = []
            for x_low in range(2):
                for y in range(NY):
                    x, which = (block // 2) * 2 + x_low, block % 2
                    at = x * 4 + y if which == 0 else lax.rem(y - pos[1] + NY, NY) * 4 + x
                    row = block * 512 + x_low * 256 + y * 64
                    copies.append(
                        pltpu.make_async_copy(
                            (a_ref, b_ref)[which].at[at],
                            weights.at[pl.ds(row, 64)],
                            sems.at[block * 8 + x_low * 4 + y],
                        )
                    )
            return copies

        @pl.when(step == 0)
        def _():
            for block in range(4):
                for copy in pieces(block):
                    copy.start()
            acc[...] = acc_in[...] if other else jnp.zeros_like(acc)

        for block in range(4):

            @pl.when(step == block)
            def _():
                for copy in pieces(block):
                    copy.wait()

        rows = weights[pl.ds(pl.multiple_of(step * 512, 512), 512), :]
        acc[...] += jnp.dot(acts_ref[...], rows, preferred_element_type=F32)
        input_ref[...] = lax.dot_general(
            grad_ref[...], rows, (((1,), (1,)), ((), ())), preferred_element_type=F32
        ).astype(BF)
        if other:

            @pl.when(step == 3)
            def _():
                layer_ref[...] = acc[...].astype(BF)

    def column(i, pos):
        core = 1 - pos[3] if other else pos[3]
        return (0, 4 * (i // 2) + 2 * core + i % 2)

    piece = pl.BlockSpec((tokens, 512), column)
    anywhere = pl.BlockSpec(memory_space=pltpu.HBM)
    scratch = [pltpu.VMEM((2048, HID), BF), pltpu.SemaphoreType.DMA((32,))]
    inputs = [acts, grads] + [b.reshape(16, 64, HID) for b in blocks]
    in_specs = [piece, whole((tokens, HID)), anywhere, anywhere]
    if other:
        inputs += carried
        in_specs += [whole((tokens, HID)), anywhere]
        outs = [((tokens, HID), BF), ((tokens, ROWS), BF)]
        scratch.append(pltpu.VMEM((tokens, HID), F32))
    else:
        outs = [((tokens, HID), F32), ((tokens, ROWS), BF)]
    return call(
        body,
        pos,
        inputs,
        in_specs,
        outs + [TOKEN],
        [whole((tokens, HID)), piece, whole((8, 128))],
        grid=(4,),
        scratch=scratch,
        flops=4 * tokens * 2048 * HID,
        vmem=56,
        after=after,
        aliases={6: 1} if other else None,
    )


def per_device(activations, output_grad, old_master, old_first, old_second, old_rows):
    micro, tokens, width = activations.shape
    hidden = output_grad.shape[2]
    acts = activations.reshape(micro * tokens, width)
    grads = output_grad.reshape(micro * tokens, hidden)
    pos = position()

    terms = [local_gradient(part, pos, acts, grads) for part in range(2)]
    got = [shifted(t.reshape(1024, HID), dcore=1) for t in terms]
    weights, state, done = outgoing(pos, old_rows, old_master, old_first, old_second, (terms[1],))
    arrived = lax.all_to_all(weights, "shard", split_axis=0, concat_axis=0, tiled=True)

    *pieces_a, done = local_gradient(0, pos, acts, grads, got[0], after=(done,))
    *pieces_b, done = local_gradient(1, pos, acts, grads, got[1], after=(done,))
    part_a, part_b, done = place_weights(pos, arrived, after=(done,))
    sum_a, sum_b = sum_rings(pos, pieces_a, pieces_b, (done,))

    block_a = gather(held_until(pos, (part_a,), sum_a[3:])[0], "x")
    state = lax.all_to_all(state, "shard", split_axis=0, concat_axis=0, tiled=True)

    own_a, one, two, three, all_b = add_first(pos, sum_a, sum_b, (state,))
    got_a = [shifted(v, dy=d + 1) for d, v in enumerate((one, two, three))]
    part_b = held_until(pos, (part_b,), got_a)[0]
    block_b = jnp.concatenate([part_b] + [shifted(part_b, dy=-d) for d in (1, 2, 3)])
    second = add_second(pos, own_a, got_a, exchange(all_b, "x"))
    total = add_third(pos, exchange(second, "z"), ())
    owned = to_owners(total)

    block_a, block_b = held_until(pos, (block_a, block_b), (total,))
    other_a, other_b = shifted(block_a, dcore=1), shifted(block_b, dcore=1)
    acc, half, done = products(False, pos, acts, grads, (block_a, block_b))
    layer_out, input_grad, done = products(True, pos, acts, grads, (other_a, other_b), (acc, half))
    new_master, new_first, new_second = adam(pos, owned, state, (done,))
    return (
        layer_out.reshape(micro, tokens, hidden),
        input_grad.reshape(micro, tokens, width),
        new_master,
        new_first,
        new_second,
    )


def solution(mesh):
    in_specs = (
        P(None, AXES, None),
        P(None, AXES, None),
        P("shard", None),
        P("shard", None),
        P("shard", None),
        P("shard"),
    )
    out_specs = (
        P(None, AXES, None),
        P(None, AXES, None),
        P("shard", None),
        P("shard", None),
        P("shard", None),
    )
    return jax.shard_map(per_device, mesh=mesh, in_specs=in_specs, out_specs=out_specs, check_vma=False)
```
